32 devices in a mesh: ctx: 16 (over z, y, core), head: 2 (over x).
Axes of the slice: x: 2, y: 2, z: 4, core: 2. Of those that a mesh axis runs over, the one named last changes fastest.
Arguments:
- queries: bfloat16 [64, 4096, 128], P(None, ('ctx', 'head')), may hold values from -6 to 6
- keys: bfloat16 [8, 4096, 128], P(None, ('ctx', 'head')), may hold values from -6 to 6
- values: bfloat16 [8, 4096, 128], P(None, ('ctx', 'head')), may hold values from -6 to 6
- delta: bfloat16 [64, 4096], P(None, ('ctx', 'head')), may hold values from -270 to 270
- grad_out: bfloat16 [64, 4096, 128], P(None, ('ctx', 'head')), may hold values from -24 to 24
- lse: bfloat16 [64, 4096], P(None, ('ctx', 'head')), may hold values from 6 to 8
Outputs:
- query_grads: bfloat16 [64, 4096, 128], P(None, ('ctx', 'head'))
- key_grads: bfloat16 [8, 4096, 128], P(None, ('ctx', 'head'))
- value_grads: bfloat16 [8, 4096, 128], P(None, ('ctx', 'head'))
The draws below stay inside these ranges and needn't reach their ends.
All inputs are finite; a program needn't handle non-finite values.
Results may differ from the reference program's by a relative error of at most 0.005.
Values may be sent and summed in bfloat16 or wider, within the bound.
A program may use at most 128 MiB of HBM per device.

```python
import math
import jax
import jax.numpy as jnp
from jax import lax

HEADS = 64
KV_HEADS = 8
HEAD_DIM = 128
BLOCK = 256
TOKENS = 4096
N_CTX = 16


def level_of(stream_key, shape, pieces, low, top_value):
    def one(dim, shards_of):
        draws = jax.random.uniform(jax.random.fold_in(jax.random.fold_in(stream_key, 6), dim), (shards_of,), jnp.float32, low / len(pieces), top_value / len(pieces))
        return jnp.repeat(jnp.exp(draws), shape[dim] // shards_of).reshape((-1,) + (1,) * (len(shape) - dim - 1))

    level = one(*pieces[0])
    for cut in pieces[1:]:
        level = level * one(*cut)
    return level


def bell_draw(rng, dims, deviation, most, shards=(), kind=jnp.bfloat16):
    values = deviation * jax.random.normal(rng, dims, jnp.float32)
    if shards:
        values = values * level_of(rng, dims, shards, -0.22, 0.18)
    return jnp.clip(values, -most, most).astype(kind)


def setup_inputs(seed: int = 0) -> dict:
    arg_keys = jax.random.split(jax.random.key(seed), 7)
    return {
        "queries": bell_draw(arg_keys[0], (HEADS, TOKENS, HEAD_DIM), 1.0, 6.0, ((1, 32),)),
        "keys": bell_draw(arg_keys[1], (KV_HEADS, TOKENS, HEAD_DIM), 1.0, 6.0, ((1, 32),)),
        "values": bell_draw(arg_keys[2], (KV_HEADS, TOKENS, HEAD_DIM), 1.0, 6.0, ((1, 32),)),
        "delta": bell_draw(arg_keys[3], (HEADS, TOKENS), (4.0 * HEAD_DIM ** 0.5), 270.0, ((1, 32),)),
        "grad_out": bell_draw(arg_keys[4], (HEADS, TOKENS, HEAD_DIM), 4.0, 24.0, ((1, 32),)),
        "lse": jnp.clip(6.0 + 2.0 * jax.random.uniform(arg_keys[5], (HEADS, TOKENS), jnp.float32) ** level_of(arg_keys[5], (HEADS, TOKENS), ((1, 32),), -0.2, 0.2), 6.0, 8.0).astype(jnp.bfloat16),
    }


def tile_grads(queries, delta, grads_out, lse, keys, values, allowed):
    heads, rows, width = queries.shape
    groups = keys.shape[0]
    ratio = heads // groups
    scale = 1.0 / math.sqrt(width)
    q_four = queries.astype(jnp.float32).reshape(groups, ratio, rows, width)
    g_four = grads_out.astype(jnp.float32).reshape(groups, ratio, rows, width)
    delta_f = delta.astype(jnp.float32).reshape(groups, ratio, rows)
    key_f = keys.astype(jnp.float32)
    val_f = values.astype(jnp.float32)
    scores = jnp.einsum('kgrd,kjd->kgrj', q_four, key_f) * scale
    probs = jnp.exp(scores - lse.astype(jnp.float32).reshape(groups, ratio, rows)[..., None])
    if allowed is not None:
        probs = jnp.where(allowed, probs, 0.0)
    probs_half = probs.astype(jnp.bfloat16).astype(jnp.float32)
    dvalue = jnp.einsum('kgrj,kgrd->kjd', probs_half, g_four)
    dprobs = jnp.einsum('kgrd,kjd->kgrj', g_four, val_f)
    dscores = (probs * (dprobs - delta_f[..., None])).astype(jnp.bfloat16).astype(jnp.float32)
    dquery = jnp.einsum('kgrj,kjd->kgrd', dscores, key_f) * scale
    dkey = jnp.einsum('kgrj,kgrd->kjd', dscores, q_four) * scale
    return (dquery.reshape(heads, rows, width), dkey, dvalue)

def reference(queries, keys, values, delta, grad_out, lse):
    blocks = N_CTX
    offset = blocks // 2
    span = BLOCK
    positions = jnp.arange(span, dtype=jnp.int32)
    causal = positions[None, :] <= positions[:, None]

    def take(array, index):
        return lax.dynamic_slice_in_dim(array, (index * span).astype(jnp.int32), span, 1)

    def one_block(index):
        far = jnp.maximum(index - offset, 0).astype(jnp.int32)
        q_blk = take(queries, index)
        d_blk = take(delta, index)
        g_blk = take(grad_out, index)
        l_blk = take(lse, index)
        dq_near, dk_near, dv_near = tile_grads(q_blk, d_blk, g_blk, l_blk, take(keys, index), take(values, index), causal)
        dq_far, dk_far, dv_far = tile_grads(q_blk, d_blk, g_blk, l_blk, take(keys, far), take(values, far), None)
        valid = (index >= offset).astype(jnp.float32)
        dq_blk = (dq_near + valid * dq_far).astype(jnp.bfloat16)
        return (dq_blk, dk_near, dv_near, valid * dk_far, valid * dv_far)
    dq_all, dk_near, dv_near, dk_far, dv_far = lax.map(one_block, jnp.arange(blocks, dtype=jnp.int32))
    dk_total = dk_near + jnp.concatenate([dk_far[offset:], jnp.zeros_like(dk_far[:blocks - offset])], 0)
    dv_total = dv_near + jnp.concatenate([dv_far[offset:], jnp.zeros_like(dv_far[:blocks - offset])], 0)

    def unblock(array):
        return jnp.transpose(array, (1, 0, 2, 3)).reshape(array.shape[1], blocks * span, array.shape[3])
    query_grads = unblock(dq_all)
    key_grads = unblock(dk_total.astype(jnp.bfloat16))
    value_grads = unblock(dv_total.astype(jnp.bfloat16))
    return (query_grads, key_grads, value_grads)
```

```python
import functools
import math

import jax
import jax.numpy as jnp
from jax import lax
from jax.experimental import pallas as pl
from jax.experimental.pallas import tpu as pltpu
from jax.sharding import PartitionSpec as P

F32 = jnp.float32
BF16 = jnp.bfloat16
MESH = pl.DeviceIdType.MESH
LOG2E = 1.0 / math.log(2.0)
NEAR, FAR, RELAY, NEAR_BACK, SWAP, FAR_BACK = range(6)


def dot(a, b, dims):
    return lax.dot_general(a, b, (dims, ((), ())), preferred_element_type=F32)


NT = ((1,), (1,))
NN = ((1,), (0,))


def kernel(
    n_ctx,
    q_hbm, k_ref, v_ref, delta_ref, g_hbm, lse_ref,
    dq_hbm, dk_ref, dv_ref,
    q_ref, g_ref, dq_ref, dq_acc, lse2, delta_f,
    own_kv, near_kv, far_kv, relay_kv,
    near_acc, far_acc,
    near_send, near_recv, swap_send, swap_recv, far_send, far_recv,
    load_sem, store_sem, send_sem, recv_sem,
):
    groups, rows, width = k_ref.shape
    heads = q_ref.shape[0]
    ratio = heads // groups
    pair = 2
    scale = 1.0 / math.sqrt(width)
    half = n_ctx // 2
    c = lax.axis_index("ctx")
    h = lax.axis_index("head")
    late = c >= half
    early = c < half
    x_dev = {"head": 1 - h}
    z_dev = {"ctx": lax.rem(c + half, n_ctx)}

    load_q = pltpu.make_async_copy(q_hbm, q_ref, load_sem.at[0])
    load_g = pltpu.make_async_copy(g_hbm, g_ref, load_sem.at[1])
    load_q.start()
    load_g.start()

    barrier = pltpu.get_barrier_semaphore()
    for dev in (x_dev, z_dev):
        pl.semaphore_signal(barrier, inc=1, device_id=dev, device_id_type=MESH)
    own_kv[:, 0] = k_ref[...]
    own_kv[:, 1] = v_ref[...]
    lse2[...] = lse_ref[...].astype(F32) * LOG2E
    delta_f[...] = delta_ref[...].astype(F32)
    pl.semaphore_wait(barrier, 2)

    def send(kind, src, dst, dev, g):
        return pltpu.make_async_remote_copy(
            src_ref=src.at[g],
            dst_ref=dst.at[g],
            send_sem=send_sem.at[kind, g],
            recv_sem=recv_sem.at[kind, g],
            device_id=dev,
            device_id_type=MESH,
        )

    def near_copy(g):
        return send(NEAR, own_kv, near_kv, x_dev, g)

    def far_copy(g):
        return send(FAR, own_kv, far_kv, z_dev, g)

    def relay_copy(g):
        return send(RELAY, far_kv, relay_kv, x_dev, g)

    def near_back(g):
        return send(NEAR_BACK, near_send, near_recv, x_dev, g)

    def swap_copy(g):
        return send(SWAP, swap_send, swap_recv, x_dev, g)

    def far_back(g):
        return send(FAR_BACK, far_send, far_recv, z_dev, g)

    ahead = 4

    @pl.when(early)
    def _():
        @pl.loop(0, groups)
        def _(g):
            far_copy(g).start()

    @pl.when(h == 0)
    def _():
        @pl.loop(0, groups)
        def _(g):
            @pl.when(early | (g < ahead))
            def _():
                near_copy(g).start()

    def unit(g, kv, diagonal, first):
        k = kv[g, 0]
        v = kv[g, 1]
        k_t = k.astype(F32).T.astype(BF16)
        dk = jnp.zeros((rows, width), F32)
        dv = jnp.zeros((rows, width), F32)
        lanes = pair * rows
        if diagonal:
            key_pos = lax.broadcasted_iota(jnp.int32, (rows, lanes), 0)
            query_pos = lax.broadcasted_iota(jnp.int32, (rows, lanes), 1) % rows
            allowed = key_pos <= query_pos
        for t in range(ratio // pair):
            head = g * ratio + t * pair
            q = q_ref[pl.ds(head, pair)].reshape(lanes, width)
            go = g_ref[pl.ds(head, pair)].reshape(lanes, width)
            lse = jnp.concatenate([lse2[pl.ds(head + i, 1), :] for i in range(pair)], 1)
            delta = jnp.concatenate([delta_f[pl.ds(head + i, 1), :] for i in range(pair)], 1)
            probs = jnp.exp2(dot(k, q, NT) * (scale * LOG2E) - lse)
            if diagonal:
                probs = jnp.where(allowed, probs, 0.0)
            dprobs = dot(v, go, NT)
            dscores = (probs * (dprobs - delta)).astype(BF16)
            dv += dot(probs.astype(BF16), go, NN)
            dk += dot(dscores, q, NN)
            dq_t = dot(k_t, dscores, NN)
            at = pl.ds(t * lanes, lanes)
            if first:
                dq_acc[g, :, at] = dq_t
            else:
                dq_acc[g, :, at] += dq_t
        return dk * scale, dv

    def finish_dq(g):
        for i in range(ratio):
            dq_t = dq_acc[g, :, pl.ds(i * rows, rows)] * scale
            dq_ref[g * ratio + i] = dq_t.T.astype(BF16)
        store_dq(g).start()

    def store_dq(g):
        at = pl.ds(g * ratio, ratio)
        return pltpu.make_async_copy(dq_ref.at[at], dq_hbm.at[at], store_sem.at[g])

    load_q.wait()
    load_g.wait()

    @pl.loop(0, groups)
    def _(g):
        dk, dv = unit(g, own_kv, True, True)
        near_acc[g, 0] = dk
        near_acc[g, 1] = dv

        @pl.when(early & (h == 0))
        def _():
            finish_dq(g)

    def near_unit(g):
        near_copy(g).wait_recv()
        dk, dv = unit(g, near_kv, False, False)
        near_send[g, 0] = dk.astype(BF16)
        near_send[g, 1] = dv.astype(BF16)
        near_back(g).start()

    @pl.when(early & (h == 1))
    def _():
        @pl.loop(0, groups)
        def _(g):
            near_unit(g)
            finish_dq(g)

    @pl.when(late)
    def _():
        @pl.loop(0, groups + 3)
        def _(t):
            @pl.when(t < groups)
            def _():
                far_copy(t).wait_recv()
                relay_copy(t).start()

                @pl.when((h == 0) & (t + ahead < groups))
                def _():
                    near_copy(t + ahead).start()

                dk, dv = unit(t, far_kv, False, False)
                far_acc[t, 0] = dk
                far_acc[t, 1] = dv

            @pl.when((t >= 1) & (t <= groups))
            def _():
                g = t - 1
                relay_copy(g).wait_recv()
                dk, dv = unit(g, relay_kv, False, False)
                swap_send[g, 0] = dk.astype(BF16)
                swap_send[g, 1] = dv.astype(BF16)
                swap_copy(g).start()
                finish_dq(g)

            @pl.when((h == 1) & (t < groups))
            def _():
                near_unit(t)

            @pl.when(t >= 3)
            def _():
                g = t - 3
                swap_copy(g).wait_recv()
                far_send[g] = (far_acc[g] + swap_recv[g].astype(F32)).astype(BF16)
                far_back(g).start()

    @pl.loop(0, groups)
    def _(g):
        @pl.when(h == 0)
        def _():
            near_back(g).wait_recv()
            near_acc[g] += near_recv[g].astype(F32)

        @pl.when(early)
        def _():
            far_back(g).wait_recv()
            near_acc[g] += far_recv[g].astype(F32)

        dk_ref[g] = near_acc[g, 0].astype(BF16)
        dv_ref[g] = near_acc[g, 1].astype(BF16)

    @pl.loop(0, groups)
    def _(g):
        store_dq(g).wait()

        @pl.when(h == 0)
        def _():
            near_copy(g).wait_send()

        @pl.when(h == 1)
        def _():
            near_back(g).wait_send()

        @pl.when(early)
        def _():
            far_copy(g).wait_send()

        @pl.when(late)
        def _():
            relay_copy(g).wait_send()
            swap_copy(g).wait_send()
            far_back(g).wait_send()


def local(queries, keys, values, delta, grad_out, lse):
    heads, rows, width = queries.shape
    groups = keys.shape[0]
    ratio = heads // groups
    n_ctx = lax.axis_size("ctx")
    block = (groups, 2, rows, width)
    vmem = pl.BlockSpec(memory_space=pltpu.VMEM)
    anywhere = pl.BlockSpec(memory_space=pl.ANY)
    return pl.pallas_call(
        functools.partial(kernel, n_ctx),
        out_shape=(
            jax.ShapeDtypeStruct(queries.shape, BF16),
            jax.ShapeDtypeStruct(keys.shape, BF16),
            jax.ShapeDtypeStruct(values.shape, BF16),
        ),
        in_specs=[anywhere, vmem, vmem, vmem, anywhere, vmem],
        out_specs=(anywhere, vmem, vmem),
        scratch_shapes=[
            pltpu.VMEM(queries.shape, BF16),
            pltpu.VMEM(queries.shape, BF16),
            pltpu.VMEM(queries.shape, BF16),
            pltpu.VMEM((groups, width, ratio * rows), F32),
            pltpu.VMEM((heads, rows), F32),
            pltpu.VMEM((heads, rows), F32),
        ]
        + [pltpu.VMEM(block, BF16)] * 4
        + [pltpu.VMEM(block, F32)] * 2
        + [pltpu.VMEM(block, BF16)] * 6
        + [
            pltpu.SemaphoreType.DMA((2,)),
            pltpu.SemaphoreType.DMA((groups,)),
            pltpu.SemaphoreType.DMA((6, groups)),
            pltpu.SemaphoreType.DMA((6, groups)),
        ],
        compiler_params=pltpu.CompilerParams(
            collective_id=0, has_side_effects=True, vmem_limit_bytes=48 * 1024 * 1024
        ),
    )(queries, keys, values, delta, grad_out, lse)


def solution(mesh):
    wide = P(None, ("ctx", "head"), None)
    flat = P(None, ("ctx", "head"))
    return jax.shard_map(
        local,
        mesh=mesh,
        in_specs=(wide, wide, wide, flat, wide, flat),
        out_specs=(wide, wide, wide),
        check_vma=False,
    )
```

```python
import functools
import math

import jax
import jax.numpy as jnp
from jax import lax
from jax.experimental import pallas as pl
from jax.experimental.pallas import tpu as pltpu
from jax.sharding import PartitionSpec as P

F32 = jnp.float32
BF16 = jnp.bfloat16
MESH = pl.DeviceIdType.MESH
LOG2E = 1.0 / math.log(2.0)
NEAR, FAR, RELAY, NEAR_BACK, SWAP, FAR_BACK = range(6)


def dot(a, b, dims):
    return lax.dot_general(a, b, (dims, ((), ())), preferred_element_type=F32)


NT = ((1,), (1,))
NN = ((1,), (0,))


def kernel(
    n_ctx,
    q_hbm, k_hbm, v_hbm, delta_hbm, g_hbm, lse_hbm,
    dq_hbm, dk_hbm, dv_hbm,
    q_ref, g_ref, dq_ref, dk_ref, dv_ref, lse_ref, delta_ref, dq_acc, lse2, delta_f,
    own_kv, near_kv, far_kv, relay_kv,
    near_acc, far_acc,
    near_send, near_recv, swap_send, swap_recv, far_send, far_recv,
    load_sem, store_sem, send_sem, recv_sem,
):
    groups, rows, width = k_hbm.shape
    heads = q_ref.shape[0]
    ratio = heads // groups
    pair = 2
    scale = 1.0 / math.sqrt(width)
    half = n_ctx // 2
    c = lax.axis_index("ctx")
    h = lax.axis_index("head")
    late = c >= half
    early = c < half
    x_dev = {"head": 1 - h}
    z_dev = {"ctx": lax.rem(c + half, n_ctx)}

    loads = [
        pltpu.make_async_copy(src, dst, load_sem.at[i])
        for i, (src, dst) in enumerate((
            (k_hbm, own_kv.at[:, 0]), (v_hbm, own_kv.at[:, 1]), (lse_hbm, lse_ref),
            (delta_hbm, delta_ref), (q_hbm, q_ref), (g_hbm, g_ref),
        ))
    ]
    for load in loads:
        load.start()

    barrier = pltpu.get_barrier_semaphore()
    for dev in (x_dev, z_dev):
        pl.semaphore_signal(barrier, inc=1, device_id=dev, device_id_type=MESH)
    loads[0].wait()
    loads[1].wait()
    pl.semaphore_wait(barrier, 2)

    def send(kind, src, dst, dev, g):
        return pltpu.make_async_remote_copy(
            src_ref=src.at[g],
            dst_ref=dst.at[g],
            send_sem=send_sem.at[kind, g],
            recv_sem=recv_sem.at[kind, g],
            device_id=dev,
            device_id_type=MESH,
        )

    def near_copy(g):
        return send(NEAR, own_kv, near_kv, x_dev, g)

    def far_copy(g):
        return send(FAR, own_kv, far_kv, z_dev, g)

    def relay_copy(g):
        return send(RELAY, far_kv, relay_kv, x_dev, g)

    def near_back(g):
        return send(NEAR_BACK, near_send, near_recv, x_dev, g)

    def swap_copy(g):
        return send(SWAP, swap_send, swap_recv, x_dev, g)

    def far_back(g):
        return send(FAR_BACK, far_send, far_recv, z_dev, g)

    ahead = 4
    lead = 2

    @pl.when(early)
    def _():
        @pl.loop(0, groups)
        def _(g):
            far_copy(g).start()

    @pl.when(h == 0)
    def _():
        @pl.loop(0, groups)
        def _(g):
            @pl.when(early | (g < ahead))
            def _():
                near_copy(g).start()

    def unit(g, blocks, diagonal, first):
        k = jnp.concatenate([kv[g, 0] for kv in blocks], 0)
        v = jnp.concatenate([kv[g, 1] for kv in blocks], 0)
        k_t = k.astype(F32).T.astype(BF16)
        keys = len(blocks) * rows
        lanes = pair * rows
        if diagonal:
            key_pos = lax.broadcasted_iota(jnp.int32, (keys, lanes), 0) - (keys - rows)
            query_pos = lax.broadcasted_iota(jnp.int32, (keys, lanes), 1) % rows
            allowed = key_pos <= query_pos
        probs_half = []
        dscores_half = []
        for t in range(ratio // pair):
            head = g * ratio + t * pair
            q = q_ref[pl.ds(head, pair)].reshape(lanes, width)
            go = g_ref[pl.ds(head, pair)].reshape(lanes, width)
            lse = jnp.concatenate([lse2[pl.ds(head + i, 1), :] for i in range(pair)], 1)
            delta = jnp.concatenate([delta_f[pl.ds(head + i, 1), :] for i in range(pair)], 1)
            probs = jnp.exp2(dot(k, q, NT) * (scale * LOG2E) - lse)
            if diagonal:
                probs = jnp.where(allowed, probs, 0.0)
            dprobs = dot(v, go, NT)
            dscores = (probs * (dprobs - delta)).astype(BF16)
            probs_half.append(probs.astype(BF16))
            dscores_half.append(dscores)
            dq_t = dot(k_t, dscores, NN)
            at = pl.ds(t * lanes, lanes)
            if first:
                dq_acc[g, :, at] = dq_t
            else:
                dq_acc[g, :, at] += dq_t
        at = pl.ds(g * ratio, ratio)
        q = q_ref[at].reshape(ratio * rows, width)
        go = g_ref[at].reshape(ratio * rows, width)
        dk = dot(jnp.concatenate(dscores_half, 1), q, NN) * scale
        dv = dot(jnp.concatenate(probs_half, 1), go, NN)
        return dk, dv

    def finish_dq(g):
        for i in range(ratio):
            dq_t = (dq_acc[g, :, pl.ds(i * rows, rows)] * scale).astype(BF16)
            dq_ref[g * ratio + i] = dq_t.T
        store_dq(g).start()

    def store_dq(g):
        at = pl.ds(g * ratio, ratio)
        return pltpu.make_async_copy(dq_ref.at[at], dq_hbm.at[at], store_sem.at[g])

    for load in loads[2:]:
        load.wait()
    lse2[...] = lse_ref[...].astype(F32) * LOG2E
    delta_f[...] = delta_ref[...].astype(F32)

    @pl.when(h == 0)
    def _():
        @pl.loop(0, groups)
        def _(g):
            dk, dv = unit(g, [own_kv], True, True)
            near_acc[g, 0] = dk
            near_acc[g, 1] = dv

            @pl.when(early)
            def _():
                finish_dq(g)

    def near_unit(g):
        near_copy(g).wait_recv()
        dk, dv = unit(g, [near_kv, own_kv], True, True)
        near_acc[g, 0] = dk[rows:]
        near_acc[g, 1] = dv[rows:]
        near_send[g, 0] = dk[:rows].astype(BF16)
        near_send[g, 1] = dv[:rows].astype(BF16)
        near_back(g).start()

    @pl.when(h == 1)
    def _():
        @pl.loop(0, jnp.where(early, groups, lead))
        def _(g):
            near_unit(g)

            @pl.when(early)
            def _():
                finish_dq(g)

    @pl.when(late)
    def _():
        @pl.loop(0, groups + 3)
        def _(t):
            @pl.when(t < groups)
            def _():
                far_copy(t).wait_recv()
                relay_copy(t).start()

                @pl.when((h == 0) & (t + ahead < groups))
                def _():
                    near_copy(t + ahead).start()

            @pl.when((t >= 1) & (t <= groups))
            def _():
                g = t - 1
                relay_copy(g).wait_recv()
                dk, dv = unit(g, [far_kv, relay_kv], False, False)
                swap_send[g, 0] = dk[rows:].astype(BF16)
                swap_send[g, 1] = dv[rows:].astype(BF16)
                swap_copy(g).start()
                far_acc[g, 0] = dk[:rows]
                far_acc[g, 1] = dv[:rows]
                finish_dq(g)

            @pl.when((h == 1) & (t + lead < groups))
            def _():
                near_unit(t + lead)

            @pl.when(t >= 3)
            def _():
                g = t - 3
                swap_copy(g).wait_recv()
                far_send[g] = (far_acc[g] + swap_recv[g].astype(F32)).astype(BF16)
                far_back(g).start()

    @pl.loop(0, groups)
    def _(g):
        @pl.when(h == 0)
        def _():
            near_back(g).wait_recv()
            near_acc[g] += near_recv[g].astype(F32)

        @pl.when(early)
        def _():
            far_back(g).wait_recv()
            near_acc[g] += far_recv[g].astype(F32)

        dk_ref[g] = near_acc[g, 0].astype(BF16)
        dv_ref[g] = near_acc[g, 1].astype(BF16)

    stores = [
        pltpu.make_async_copy(dk_ref, dk_hbm, load_sem.at[0]),
        pltpu.make_async_copy(dv_ref, dv_hbm, load_sem.at[1]),
    ]
    for store in stores:
        store.start()

    @pl.loop(0, groups)
    def _(g):
        store_dq(g).wait()

        @pl.when(h == 0)
        def _():
            near_copy(g).wait_send()

        @pl.when(h == 1)
        def _():
            near_back(g).wait_send()

        @pl.when(early)
        def _():
            far_copy(g).wait_send()

        @pl.when(late)
        def _():
            relay_copy(g).wait_send()
            swap_copy(g).wait_send()
            far_back(g).wait_send()

    for store in stores:
        store.wait()


def write_out(*refs):
    sem = refs[-1]
    count = len(refs) // 2
    copies = [
        pltpu.make_async_copy(refs[i], refs[count + i], sem.at[i]) for i in range(count)
    ]
    for copy in copies:
        copy.start()
    for copy in copies:
        copy.wait()


def local(queries, keys, values, delta, grad_out, lse):
    heads, rows, width = queries.shape
    groups = keys.shape[0]
    ratio = heads // groups
    n_ctx = lax.axis_size("ctx")
    block = (groups, 2, rows, width)
    anywhere = pl.BlockSpec(memory_space=pl.ANY)
    grads = pl.pallas_call(
        functools.partial(kernel, n_ctx),
        out_shape=(
            jax.ShapeDtypeStruct(queries.shape, BF16),
            jax.ShapeDtypeStruct(keys.shape, BF16),
            jax.ShapeDtypeStruct(values.shape, BF16),
        ),
        in_specs=[anywhere] * 6,
        out_specs=(anywhere,) * 3,
        scratch_shapes=[
            pltpu.VMEM(queries.shape, BF16),
            pltpu.VMEM(queries.shape, BF16),
            pltpu.VMEM(queries.shape, BF16),
            pltpu.VMEM(keys.shape, BF16),
            pltpu.VMEM(keys.shape, BF16),
            pltpu.VMEM(lse.shape, BF16),
            pltpu.VMEM(lse.shape, BF16),
            pltpu.VMEM((groups, width, ratio * rows), F32),
            pltpu.VMEM((heads, rows), F32),
            pltpu.VMEM((heads, rows), F32),
        ]
        + [pltpu.VMEM(block, BF16)] * 4
        + [pltpu.VMEM(block, F32)] * 2
        + [pltpu.VMEM(block, BF16)] * 6
        + [
            pltpu.SemaphoreType.DMA((6,)),
            pltpu.SemaphoreType.DMA((groups,)),
            pltpu.SemaphoreType.DMA((6, groups)),
            pltpu.SemaphoreType.DMA((6, groups)),
        ],
        compiler_params=pltpu.CompilerParams(
            collective_id=0, has_side_effects=True, vmem_limit_bytes=60 * 1024 * 1024
        ),
    )(queries, keys, values, delta, grad_out, lse)
    return pl.pallas_call(
        write_out,
        out_shape=tuple(jax.ShapeDtypeStruct(x.shape, x.dtype) for x in grads),
        in_specs=[anywhere] * 3,
        out_specs=(anywhere,) * 3,
        scratch_shapes=[pltpu.SemaphoreType.DMA((3,))],
        compiler_params=pltpu.CompilerParams(vmem_limit_bytes=60 * 1024 * 1024),
    )(*grads)


def solution(mesh):
    wide = P(None, ("ctx", "head"), None)
    flat = P(None, ("ctx", "head"))
    return jax.shard_map(
        local,
        mesh=mesh,
        in_specs=(wide, wide, wide, flat, wide, flat),
        out_specs=(wide, wide, wide),
        check_vma=False,
    )
```

```python
import functools
import math

import jax
import jax.numpy as jnp
from jax import lax
from jax.experimental import pallas as pl
from jax.experimental.pallas import tpu as pltpu
from jax.sharding import PartitionSpec as P

F32 = jnp.float32
BF16 = jnp.bfloat16
MESH = pl.DeviceIdType.MESH
LOG2E = 1.0 / math.log(2.0)
KINDS = 7
NEAR, FAR, RELAY, NEAR_BACK, SWAP, FAR_BACK, OTHER = range(KINDS)


def dot(a, b, dims):
    return lax.dot_general(a, b, (dims, ((), ())), preferred_element_type=F32)


NT = ((1,), (1,))
NN = ((1,), (0,))


def kernel(
    n_ctx,
    q_hbm, k_hbm, v_hbm, delta_hbm, g_hbm, lse_hbm,
    dq_hbm, dk_hbm, dv_hbm,
    q_ref, g_ref, dq_ref, dk_ref, dv_ref, lse_ref, delta_ref, dq_acc, lse2, delta_f,
    own_kv, near_kv, far_kv, relay_kv,
    near_acc, far_acc,
    near_send, near_recv, swap_send, swap_recv, far_send, far_recv,
    load_sem, store_sem, send_sem, recv_sem,
):
    groups, rows, width = k_hbm.shape
    heads = q_ref.shape[0]
    ratio = heads // groups
    pair = 2
    scale = 1.0 / math.sqrt(width)
    half = n_ctx // 2
    c = lax.axis_index("ctx")
    h = lax.axis_index("head")
    late = c >= half
    early = c < half
    x_dev = {"head": 1 - h}
    z_dev = {"ctx": lax.rem(c + half, n_ctx)}

    loads = [
        pltpu.make_async_copy(src, dst, load_sem.at[i])
        for i, (src, dst) in enumerate((
            (k_hbm, own_kv.at[:, 0]), (v_hbm, own_kv.at[:, 1]), (lse_hbm, lse_ref),
            (delta_hbm, delta_ref), (q_hbm, q_ref), (g_hbm, g_ref),
        ))
    ]
    for load in loads:
        load.start()

    barrier = pltpu.get_barrier_semaphore()
    for dev in (x_dev, z_dev):
        pl.semaphore_signal(barrier, inc=1, device_id=dev, device_id_type=MESH)
    loads[0].wait()
    loads[1].wait()
    pl.semaphore_wait(barrier, 2)

    def send(kind, src, dst, dev, g):
        return pltpu.make_async_remote_copy(
            src_ref=src.at[g],
            dst_ref=dst.at[g],
            send_sem=send_sem.at[kind, g],
            recv_sem=recv_sem.at[kind, g],
            device_id=dev,
            device_id_type=MESH,
        )

    def near_copy(g):
        return send(NEAR, own_kv, near_kv, x_dev, g)

    def far_copy(g):
        return send(FAR, own_kv, far_kv, z_dev, g)

    def relay_copy(g):
        return send(RELAY, far_kv, relay_kv, x_dev, g)

    def near_back(g):
        return send(NEAR_BACK, near_send, near_recv, x_dev, g)

    def swap_copy(g):
        return send(SWAP, swap_send, swap_recv, x_dev, g)

    def far_back(g):
        return send(FAR_BACK, far_send, far_recv, z_dev, g)

    ahead = 4
    lead = 2

    def around_copy(g):
        return send(RELAY, near_kv, relay_kv, z_dev, g)

    def other_back(g):
        return send(OTHER, swap_send, relay_kv, z_dev, g)

    def other_swap(g):
        return send(SWAP, relay_kv, swap_recv, x_dev, g)

    def by_early(g):
        return lax.rem(g, 3) == 2

    def back_apart(g):
        return lax.rem(g, 4) == 0

    @pl.when(early)
    def _():
        @pl.loop(0, groups)
        def _(g):
            @pl.when(by_early(g))
            def _():
                near_copy(g).start()

        @pl.loop(0, groups)
        def _(g):
            far_copy(g).start()

            @pl.when((h == 0) & jnp.logical_not(by_early(g)))
            def _():
                near_copy(g).start()

            @pl.when(by_early(g))
            def _():
                near_copy(g).wait_recv()
                around_copy(g).start()

    @pl.when(late & (h == 0))
    def _():
        @pl.loop(0, ahead)
        def _(g):
            near_copy(g).start()

    def unit(g, blocks, diagonal, first):
        k = jnp.concatenate([kv[g, 0] for kv in blocks], 0)
        v = jnp.concatenate([kv[g, 1] for kv in blocks], 0)
        k_t = k.astype(F32).T.astype(BF16)
        keys = len(blocks) * rows
        lanes = pair * rows
        if diagonal:
            key_pos = lax.broadcasted_iota(jnp.int32, (keys, lanes), 0) - (keys - rows)
            query_pos = lax.broadcasted_iota(jnp.int32, (keys, lanes), 1) % rows
            allowed = key_pos <= query_pos
        probs_half = []
        dscores_half = []
        for t in range(ratio // pair):
            head = g * ratio + t * pair
            q = q_ref[pl.ds(head, pair)].reshape(lanes, width)
            go = g_ref[pl.ds(head, pair)].reshape(lanes, width)
            lse = jnp.concatenate([lse2[pl.ds(head + i, 1), :] for i in range(pair)], 1)
            delta = jnp.concatenate([delta_f[pl.ds(head + i, 1), :] for i in range(pair)], 1)
            probs = jnp.exp2(dot(k, q, NT) * (scale * LOG2E) - lse)
            if diagonal:
                probs = jnp.where(allowed, probs, 0.0)
            dprobs = dot(v, go, NT)
            dscores = (probs * (dprobs - delta)).astype(BF16)
            probs_half.append(probs.astype(BF16))
            dscores_half.append(dscores)
            dq_t = dot(k_t, dscores, NN)
            at = pl.ds(t * lanes, lanes)
            if first:
                dq_acc[g, :, at] = dq_t
            else:
                dq_acc[g, :, at] += dq_t
        at = pl.ds(g * ratio, ratio)
        q = q_ref[at].reshape(ratio * rows, width)
        go = g_ref[at].reshape(ratio * rows, width)
        dk = dot(jnp.concatenate(dscores_half, 1), q, NN) * scale
        dv = dot(jnp.concatenate(probs_half, 1), go, NN)
        return dk, dv

    def finish_dq(g):
        for i in range(ratio):
            dq_t = (dq_acc[g, :, pl.ds(i * rows, rows)] * scale).astype(BF16)
            dq_ref[g * ratio + i] = dq_t.T
        store_dq(g).start()

    def store_dq(g):
        at = pl.ds(g * ratio, ratio)
        return pltpu.make_async_copy(dq_ref.at[at], dq_hbm.at[at], store_sem.at[g])

    for load in loads[2:]:
        load.wait()
    lse2[...] = lse_ref[...].astype(F32) * LOG2E
    delta_f[...] = delta_ref[...].astype(F32)

    @pl.when(h == 0)
    def _():
        @pl.loop(0, groups)
        def _(g):
            dk, dv = unit(g, [own_kv], True, True)
            near_acc[g, 0] = dk
            near_acc[g, 1] = dv

            @pl.when(early)
            def _():
                finish_dq(g)

    def near_unit(g):
        @pl.when(late | jnp.logical_not(by_early(g)))
        def _():
            near_copy(g).wait_recv()

        dk, dv = unit(g, [near_kv, own_kv], True, True)
        near_acc[g, 0] = dk[rows:]
        near_acc[g, 1] = dv[rows:]
        near_send[g, 0] = dk[:rows].astype(BF16)
        near_send[g, 1] = dv[:rows].astype(BF16)
        near_back(g).start()

    @pl.when(h == 1)
    def _():
        @pl.loop(0, jnp.where(early, groups, lead))
        def _(g):
            near_unit(g)

            @pl.when(early)
            def _():
                finish_dq(g)

    @pl.when(late)
    def _():
        @pl.loop(0, groups + 3)
        def _(t):
            @pl.when(t < groups)
            def _():
                far_copy(t).wait_recv()

                @pl.when(jnp.logical_not(by_early(t)))
                def _():
                    relay_copy(t).start()

                @pl.when((h == 0) & (t + ahead < groups))
                def _():
                    near_copy(t + ahead).start()

            @pl.when((t >= 1) & (t <= groups))
            def _():
                g = t - 1
                relay_copy(g).wait_recv()
                dk, dv = unit(g, [far_kv, relay_kv], False, False)
                swap_send[g, 0] = dk[rows:].astype(BF16)
                swap_send[g, 1] = dv[rows:].astype(BF16)

                @pl.when(back_apart(g))
                def _():
                    other_back(g).start()
                    far_send[g, 0] = dk[:rows].astype(BF16)
                    far_send[g, 1] = dv[:rows].astype(BF16)
                    far_back(g).start()

                @pl.when(jnp.logical_not(back_apart(g)))
                def _():
                    swap_copy(g).start()
                    far_acc[g, 0] = dk[:rows]
                    far_acc[g, 1] = dv[:rows]

                finish_dq(g)

            @pl.when((h == 1) & (t + lead < groups))
            def _():
                near_unit(t + lead)

            @pl.when((t >= 3) & jnp.logical_not(back_apart(t - 3)))
            def _():
                g = t - 3
                swap_copy(g).wait_recv()
                far_send[g] = (far_acc[g] + swap_recv[g].astype(F32)).astype(BF16)
                far_back(g).start()

    @pl.when(early)
    def _():
        @pl.loop(0, groups)
        def _(g):
            @pl.when(back_apart(g))
            def _():
                other_back(g).wait_recv()
                other_swap(g).start()

    @pl.loop(0, groups)
    def _(g):
        @pl.when(h == 0)
        def _():
            near_back(g).wait_recv()
            near_acc[g] += near_recv[g].astype(F32)

        @pl.when(early)
        def _():
            far_back(g).wait_recv()
            near_acc[g] += far_recv[g].astype(F32)

            @pl.when(back_apart(g))
            def _():
                other_swap(g).wait_recv()
                near_acc[g] += swap_recv[g].astype(F32)

        dk_ref[g] = near_acc[g, 0].astype(BF16)
        dv_ref[g] = near_acc[g, 1].astype(BF16)

    stores = [
        pltpu.make_async_copy(dk_ref, dk_hbm, load_sem.at[0]),
        pltpu.make_async_copy(dv_ref, dv_hbm, load_sem.at[1]),
    ]
    for store in stores:
        store.start()

    @pl.loop(0, groups)
    def _(g):
        store_dq(g).wait()

        @pl.when((h == 0) | (early & by_early(g)))
        def _():
            near_copy(g).wait_send()

        @pl.when(h == 1)
        def _():
            near_back(g).wait_send()

        @pl.when(early)
        def _():
            far_copy(g).wait_send()

        @pl.when(early & by_early(g))
        def _():
            around_copy(g).wait_send()

        @pl.when(early & back_apart(g))
        def _():
            other_swap(g).wait_send()

        @pl.when(late)
        def _():
            far_back(g).wait_send()

        @pl.when(late & jnp.logical_not(by_early(g)))
        def _():
            relay_copy(g).wait_send()

        @pl.when(late & back_apart(g))
        def _():
            other_back(g).wait_send()

        @pl.when(late & jnp.logical_not(back_apart(g)))
        def _():
            swap_copy(g).wait_send()

    for store in stores:
        store.wait()


def write_out(parts, *refs):
    count = len(parts)
    sources, results, staged = refs[:count], refs[count:2 * count], refs[2 * count:3 * count]
    read_sem, write_sem = refs[3 * count:]
    reads, writes = [], []
    for i, cuts in enumerate(parts):
        size = sources[i].shape[0] // cuts
        for j in range(cuts):
            at = pl.ds(j * size, size)
            n = len(reads)
            reads.append(
                pltpu.make_async_copy(sources[i].at[at], staged[i].at[at], read_sem.at[n])
            )
            writes.append(
                pltpu.make_async_copy(staged[i].at[at], results[i].at[at], write_sem.at[n])
            )
    for read in reads:
        read.start()
    for read, write in zip(reads, writes):
        read.wait()
        write.start()
    for write in writes:
        write.wait()


def local(queries, keys, values, delta, grad_out, lse):
    heads, rows, width = queries.shape
    groups = keys.shape[0]
    ratio = heads // groups
    n_ctx = lax.axis_size("ctx")
    block = (groups, 2, rows, width)
    anywhere = pl.BlockSpec(memory_space=pl.ANY)
    grads = pl.pallas_call(
        functools.partial(kernel, n_ctx),
        out_shape=(
            jax.ShapeDtypeStruct(queries.shape, BF16),
            jax.ShapeDtypeStruct(keys.shape, BF16),
            jax.ShapeDtypeStruct(values.shape, BF16),
        ),
        in_specs=[anywhere] * 6,
        out_specs=(anywhere,) * 3,
        scratch_shapes=[
            pltpu.VMEM(queries.shape, BF16),
            pltpu.VMEM(queries.shape, BF16),
            pltpu.VMEM(queries.shape, BF16),
            pltpu.VMEM(keys.shape, BF16),
            pltpu.VMEM(keys.shape, BF16),
            pltpu.VMEM(lse.shape, BF16),
            pltpu.VMEM(lse.shape, BF16),
            pltpu.VMEM((groups, width, ratio * rows), F32),
            pltpu.VMEM((heads, rows), F32),
            pltpu.VMEM((heads, rows), F32),
        ]
        + [pltpu.VMEM(block, BF16)] * 4
        + [pltpu.VMEM(block, F32)] * 2
        + [pltpu.VMEM(block, BF16)] * 6
        + [
            pltpu.SemaphoreType.DMA((6,)),
            pltpu.SemaphoreType.DMA((groups,)),
            pltpu.SemaphoreType.DMA((KINDS, groups)),
            pltpu.SemaphoreType.DMA((KINDS, groups)),
        ],
        compiler_params=pltpu.CompilerParams(
            collective_id=0, has_side_effects=True, vmem_limit_bytes=60 * 1024 * 1024
        ),
    )(queries, keys, values, delta, grad_out, lse)
    parts = (4, 1, 1)
    return pl.pallas_call(
        functools.partial(write_out, parts),
        out_shape=tuple(jax.ShapeDtypeStruct(x.shape, x.dtype) for x in grads),
        in_specs=[anywhere] * 3,
        out_specs=(anywhere,) * 3,
        scratch_shapes=[pltpu.VMEM(x.shape, x.dtype) for x in grads]
        + [pltpu.SemaphoreType.DMA((sum(parts),))] * 2,
        compiler_params=pltpu.CompilerParams(vmem_limit_bytes=60 * 1024 * 1024),
    )(*grads)


def solution(mesh):
    wide = P(None, ("ctx", "head"), None)
    flat = P(None, ("ctx", "head"))
    return jax.shard_map(
        local,
        mesh=mesh,
        in_specs=(wide, wide, wide, flat, wide, flat),
        out_specs=(wide, wide, wide),
        check_vma=False,
    )
```

```python
import functools
import math

import jax
import jax.numpy as jnp
from jax import lax
from jax.experimental import pallas as pl
from jax.experimental.pallas import tpu as pltpu
from jax.sharding import PartitionSpec as P

F32 = jnp.float32
BF16 = jnp.bfloat16
MESH = pl.DeviceIdType.MESH
LOG2E = 1.0 / math.log(2.0)
KINDS = 7
NEAR, FAR, RELAY, NEAR_BACK, SWAP, FAR_BACK, OTHER = range(KINDS)


def dot(a, b, dims):
    return lax.dot_general(a, b, (dims, ((), ())), preferred_element_type=F32)


NT = ((1,), (1,))
NN = ((1,), (0,))


def kernel(
    n_ctx,
    q_hbm, k_hbm, v_hbm, delta_hbm, g_hbm, lse_hbm,
    dq_hbm, dk_hbm, dv_hbm,
    q_ref, g_ref, dq_ref, dk_ref, dv_ref, lse_ref, delta_ref, dq_acc, lse2, delta_f,
    own_kv, near_kv, far_kv, relay_kv,
    near_acc, far_acc,
    near_send, near_recv, swap_send, swap_recv, far_send, far_recv,
    load_sem, store_sem, send_sem, recv_sem,
):
    groups, rows, width = k_hbm.shape
    heads = q_ref.shape[0]
    ratio = heads // groups
    pair = 2
    scale = 1.0 / math.sqrt(width)
    half = n_ctx // 2
    c = lax.axis_index("ctx")
    h = lax.axis_index("head")
    late = c >= half
    early = c < half
    x_dev = {"head": 1 - h}
    z_dev = {"ctx": lax.rem(c + half, n_ctx)}

    loads = [
        pltpu.make_async_copy(src, dst, load_sem.at[i])
        for i, (src, dst) in enumerate((
            (k_hbm, own_kv.at[:, 0]), (v_hbm, own_kv.at[:, 1]), (lse_hbm, lse_ref),
            (delta_hbm, delta_ref), (q_hbm, q_ref), (g_hbm, g_ref),
        ))
    ]
    for load in loads:
        load.start()

    barrier = pltpu.get_barrier_semaphore()
    for dev in (x_dev, z_dev):
        pl.semaphore_signal(barrier, inc=1, device_id=dev, device_id_type=MESH)
    loads[0].wait()
    loads[1].wait()
    pl.semaphore_wait(barrier, 2)

    def send(kind, src, dst, dev, g):
        return pltpu.make_async_remote_copy(
            src_ref=src.at[g],
            dst_ref=dst.at[g],
            send_sem=send_sem.at[kind, g],
            recv_sem=recv_sem.at[kind, g],
            device_id=dev,
            device_id_type=MESH,
        )

    def near_copy(g):
        return send(NEAR, own_kv, near_kv, x_dev, g)

    def far_copy(g):
        return send(FAR, own_kv, far_kv, z_dev, g)

    def relay_copy(g):
        return send(RELAY, far_kv, relay_kv, x_dev, g)

    def near_back(g):
        return send(NEAR_BACK, near_send, near_recv, x_dev, g)

    def swap_copy(g):
        return send(SWAP, swap_send, swap_recv, x_dev, g)

    def far_back(g):
        return send(FAR_BACK, far_send, far_recv, z_dev, g)

    ahead = 3
    lead = 2
    flying = 2

    def around_copy(g):
        return send(RELAY, near_kv, relay_kv, z_dev, g)

    def other_back(g):
        return send(OTHER, swap_send, relay_kv, z_dev, g)

    def other_swap(g):
        return send(SWAP, relay_kv, swap_recv, x_dev, g)

    def by_early(g):
        return lax.rem(g, 3) == 2

    def back_apart(g):
        return lax.rem(g, 4) == 0

    def issue(g):
        far_copy(g).start()

        @pl.when(by_early(g))
        def _():
            near_copy(g).wait_recv()
            around_copy(g).start()

    @pl.when(early)
    def _():
        @pl.loop(0, groups)
        def _(g):
            @pl.when(by_early(g) | ((h == 0) & (g == 0)))
            def _():
                near_copy(g).start()

        @pl.loop(0, flying)
        def _(g):
            issue(g)

    @pl.when(late & (h == 0))
    def _():
        @pl.loop(0, ahead)
        def _(g):
            near_copy(g).start()

    def unit(g, blocks, diagonal, first):
        k = jnp.concatenate([kv[g, 0] for kv in blocks], 0)
        v = jnp.concatenate([kv[g, 1] for kv in blocks], 0)
        k_t = k.astype(F32).T.astype(BF16)
        keys = len(blocks) * rows
        lanes = pair * rows
        if diagonal:
            key_pos = lax.broadcasted_iota(jnp.int32, (keys, lanes), 0) - (keys - rows)
            query_pos = lax.broadcasted_iota(jnp.int32, (keys, lanes), 1) % rows
            allowed = key_pos <= query_pos
        probs_half = []
        dscores_half = []
        for t in range(ratio // pair):
            head = g * ratio + t * pair
            q = q_ref[pl.ds(head, pair)].reshape(lanes, width)
            go = g_ref[pl.ds(head, pair)].reshape(lanes, width)
            lse = jnp.concatenate([lse2[pl.ds(head + i, 1), :] for i in range(pair)], 1)
            delta = jnp.concatenate([delta_f[pl.ds(head + i, 1), :] for i in range(pair)], 1)
            probs = jnp.exp2(dot(k, q, NT) * (scale * LOG2E) - lse)
            if diagonal:
                probs = jnp.where(allowed, probs, 0.0)
            dprobs = dot(v, go, NT)
            dscores = (probs * (dprobs - delta)).astype(BF16)
            probs_half.append(probs.astype(BF16))
            dscores_half.append(dscores)
            dq_t = dot(k_t, dscores, NN)
            at = pl.ds(t * lanes, lanes)
            if first:
                dq_acc[g, :, at] = dq_t
            else:
                dq_acc[g, :, at] += dq_t
        at = pl.ds(g * ratio, ratio)
        q = q_ref[at].reshape(ratio * rows, width)
        go = g_ref[at].reshape(ratio * rows, width)
        dk = dot(jnp.concatenate(dscores_half, 1), q, NN) * scale
        dv = dot(jnp.concatenate(probs_half, 1), go, NN)
        return dk, dv

    def finish_dq(g):
        for i in range(ratio):
            dq_t = (dq_acc[g, :, pl.ds(i * rows, rows)] * scale).astype(BF16)
            dq_ref[g * ratio + i] = dq_t.T
        store_dq(g).start()

    def store_dq(g):
        at = pl.ds(g * ratio, ratio)
        return pltpu.make_async_copy(dq_ref.at[at], dq_hbm.at[at], store_sem.at[g])

    for load in loads[2:]:
        load.wait()
    lse2[...] = lse_ref[...].astype(F32) * LOG2E
    delta_f[...] = delta_ref[...].astype(F32)

    def near_unit(g):
        @pl.when(late | jnp.logical_not(by_early(g)))
        def _():
            near_copy(g).wait_recv()

        dk, dv = unit(g, [near_kv, own_kv], True, True)
        near_acc[g, 0] = dk[rows:]
        near_acc[g, 1] = dv[rows:]
        near_send[g, 0] = dk[:rows].astype(BF16)
        near_send[g, 1] = dv[:rows].astype(BF16)
        near_back(g).start()

    def near_step(g):
        @pl.when(h == 0)
        def _():
            dk, dv = unit(g, [own_kv], True, True)
            near_acc[g, 0] = dk
            near_acc[g, 1] = dv

        @pl.when(h == 1)
        def _():
            near_unit(g)

    @pl.when(early)
    def _():
        @pl.loop(0, groups)
        def _(g):
            far_copy(g).wait_send()

            @pl.when(by_early(g))
            def _():
                around_copy(g).wait_send()

            @pl.when(g + flying < groups)
            def _():
                issue(g + flying)

            @pl.when((h == 0) & (g + 1 < groups) & jnp.logical_not(by_early(g + 1)))
            def _():
                near_copy(g + 1).start()

            near_step(g)
            finish_dq(g)

    @pl.when(late)
    def _():
        @pl.loop(0, lead)
        def _(g):
            near_step(g)

    @pl.when(late)
    def _():
        @pl.loop(0, groups + 3)
        def _(t):
            @pl.when(t < groups)
            def _():
                far_copy(t).wait_recv()

                @pl.when(jnp.logical_not(by_early(t)))
                def _():
                    relay_copy(t).start()

                @pl.when((h == 0) & (t + ahead < groups))
                def _():
                    near_copy(t + ahead).start()

            @pl.when((t >= 1) & (t <= groups))
            def _():
                g = t - 1
                relay_copy(g).wait_recv()
                dk, dv = unit(g, [far_kv, relay_kv], False, False)
                swap_send[g, 0] = dk[rows:].astype(BF16)
                swap_send[g, 1] = dv[rows:].astype(BF16)

                @pl.when(back_apart(g))
                def _():
                    other_back(g).start()
                    far_send[g, 0] = dk[:rows].astype(BF16)
                    far_send[g, 1] = dv[:rows].astype(BF16)
                    far_back(g).start()

                @pl.when(jnp.logical_not(back_apart(g)))
                def _():
                    swap_copy(g).start()
                    far_acc[g, 0] = dk[:rows]
                    far_acc[g, 1] = dv[:rows]

                finish_dq(g)

            @pl.when(t + lead < groups)
            def _():
                near_step(t + lead)

            @pl.when((t >= 3) & jnp.logical_not(back_apart(t - 3)))
            def _():
                g = t - 3
                swap_copy(g).wait_recv()
                far_send[g] = (far_acc[g] + swap_recv[g].astype(F32)).astype(BF16)
                far_back(g).start()

    @pl.when(early)
    def _():
        @pl.loop(0, groups)
        def _(g):
            @pl.when(back_apart(g))
            def _():
                other_back(g).wait_recv()
                other_swap(g).start()

    @pl.loop(0, groups)
    def _(g):
        @pl.when(h == 0)
        def _():
            near_back(g).wait_recv()
            near_acc[g] += near_recv[g].astype(F32)

        @pl.when(early)
        def _():
            far_back(g).wait_recv()
            near_acc[g] += far_recv[g].astype(F32)

            @pl.when(back_apart(g))
            def _():
                other_swap(g).wait_recv()
                near_acc[g] += swap_recv[g].astype(F32)

        dk_ref[g] = near_acc[g, 0].astype(BF16)
        dv_ref[g] = near_acc[g, 1].astype(BF16)

    stores = [
        pltpu.make_async_copy(dk_ref, dk_hbm, load_sem.at[0]),
        pltpu.make_async_copy(dv_ref, dv_hbm, load_sem.at[1]),
    ]
    for store in stores:
        store.start()

    @pl.loop(0, groups)
    def _(g):
        store_dq(g).wait()

        @pl.when((h == 0) | (early & by_early(g)))
        def _():
            near_copy(g).wait_send()

        @pl.when(h == 1)
        def _():
            near_back(g).wait_send()

        @pl.when(early & back_apart(g))
        def _():
            other_swap(g).wait_send()

        @pl.when(late)
        def _():
            far_back(g).wait_send()

        @pl.when(late & jnp.logical_not(by_early(g)))
        def _():
            relay_copy(g).wait_send()

        @pl.when(late & back_apart(g))
        def _():
            other_back(g).wait_send()

        @pl.when(late & jnp.logical_not(back_apart(g)))
        def _():
            swap_copy(g).wait_send()

    for store in stores:
        store.wait()


def write_out(parts, *refs):
    count = len(parts)
    sources, results, staged = refs[:count], refs[count:2 * count], refs[2 * count:3 * count]
    read_sem, write_sem = refs[3 * count:]
    reads, writes = [], []
    for i, cuts in enumerate(parts):
        size = sources[i].shape[0] // cuts
        for j in range(cuts):
            at = pl.ds(j * size, size)
            n = len(reads)
            reads.append(
                pltpu.make_async_copy(sources[i].at[at], staged[i].at[at], read_sem.at[n])
            )
            writes.append(
                pltpu.make_async_copy(staged[i].at[at], results[i].at[at], write_sem.at[n])
            )
    for read in reads:
        read.start()
    for read, write in zip(reads, writes):
        read.wait()
        write.start()
    for write in writes:
        write.wait()


def local(queries, keys, values, delta, grad_out, lse):
    heads, rows, width = queries.shape
    groups = keys.shape[0]
    ratio = heads // groups
    n_ctx = lax.axis_size("ctx")
    block = (groups, 2, rows, width)
    anywhere = pl.BlockSpec(memory_space=pl.ANY)
    grads = pl.pallas_call(
        functools.partial(kernel, n_ctx),
        out_shape=(
            jax.ShapeDtypeStruct(queries.shape, BF16),
            jax.ShapeDtypeStruct(keys.shape, BF16),
            jax.ShapeDtypeStruct(values.shape, BF16),
        ),
        in_specs=[anywhere] * 6,
        out_specs=(anywhere,) * 3,
        scratch_shapes=[
            pltpu.VMEM(queries.shape, BF16),
            pltpu.VMEM(queries.shape, BF16),
            pltpu.VMEM(queries.shape, BF16),
            pltpu.VMEM(keys.shape, BF16),
            pltpu.VMEM(keys.shape, BF16),
            pltpu.VMEM(lse.shape, BF16),
            pltpu.VMEM(lse.shape, BF16),
            pltpu.VMEM((groups, width, ratio * rows), F32),
            pltpu.VMEM((heads, rows), F32),
            pltpu.VMEM((heads, rows), F32),
        ]
        + [pltpu.VMEM(block, BF16)] * 4
        + [pltpu.VMEM(block, F32)] * 2
        + [pltpu.VMEM(block, BF16)] * 6
        + [
            pltpu.SemaphoreType.DMA((6,)),
            pltpu.SemaphoreType.DMA((groups,)),
            pltpu.SemaphoreType.DMA((KINDS, groups)),
            pltpu.SemaphoreType.DMA((KINDS, groups)),
        ],
        compiler_params=pltpu.CompilerParams(
            collective_id=0, has_side_effects=True, vmem_limit_bytes=60 * 1024 * 1024
        ),
    )(queries, keys, values, delta, grad_out, lse)
    parts = (4, 1, 1)
    return pl.pallas_call(
        functools.partial(write_out, parts),
        out_shape=tuple(jax.ShapeDtypeStruct(x.shape, x.dtype) for x in grads),
        in_specs=[anywhere] * 3,
        out_specs=(anywhere,) * 3,
        scratch_shapes=[pltpu.VMEM(x.shape, x.dtype) for x in grads]
        + [pltpu.SemaphoreType.DMA((sum(parts),))] * 2,
        compiler_params=pltpu.CompilerParams(vmem_limit_bytes=60 * 1024 * 1024),
    )(*grads)


def solution(mesh):
    wide = P(None, ("ctx", "head"), None)
    flat = P(None, ("ctx", "head"))
    return jax.shard_map(
        local,
        mesh=mesh,
        in_specs=(wide, wide, wide, flat, wide, flat),
        out_specs=(wide, wide, wide),
        check_vma=False,
    )
```

```python
import functools
import math

import jax
import jax.numpy as jnp
from jax import lax
from jax.experimental import pallas as pl
from jax.experimental.pallas import tpu as pltpu
from jax.sharding import PartitionSpec as P

F32 = jnp.float32
BF16 = jnp.bfloat16
MESH = pl.DeviceIdType.MESH
LOG2E = 1.0 / math.log(2.0)
KINDS = 7
NEAR, FAR, RELAY, NEAR_BACK, SWAP, FAR_BACK, OTHER = range(KINDS)


def dot(a, b, dims):
    return lax.dot_general(a, b, (dims, ((), ())), preferred_element_type=F32)


NT = ((1,), (1,))
NN = ((1,), (0,))


def kernel(
    n_ctx,
    q_hbm, k_hbm, v_hbm, delta_hbm, g_hbm, lse_hbm,
    dq_hbm, dk_hbm, dv_hbm,
    q_ref, g_ref, dq_ref, dk_ref, dv_ref, lse_ref, delta_ref, dq_acc, lse2, delta_f,
    own_kv, near_kv, far_kv, relay_kv,
    near_acc, far_acc,
    near_send, near_recv, swap_send, swap_recv, far_send, far_recv,
    load_sem, store_sem, send_sem, recv_sem,
):
    groups, rows, width = k_hbm.shape
    heads = q_ref.shape[0]
    ratio = heads // groups
    pair = 2
    scale = 1.0 / math.sqrt(width)
    half = n_ctx // 2
    c = lax.axis_index("ctx")
    h = lax.axis_index("head")
    late = c >= half
    early = c < half
    x_dev = {"head": 1 - h}
    z_dev = {"ctx": lax.rem(c + half, n_ctx)}

    loads = [
        pltpu.make_async_copy(src, dst, load_sem.at[i])
        for i, (src, dst) in enumerate((
            (k_hbm, own_kv.at[:, 0]), (v_hbm, own_kv.at[:, 1]), (lse_hbm, lse_ref),
            (delta_hbm, delta_ref), (q_hbm, q_ref), (g_hbm, g_ref),
        ))
    ]
    for load in loads:
        load.start()

    barrier = pltpu.get_barrier_semaphore()
    for dev in (x_dev, z_dev):
        pl.semaphore_signal(barrier, inc=1, device_id=dev, device_id_type=MESH)
    loads[0].wait()
    loads[1].wait()
    pl.semaphore_wait(barrier, 2)

    def send(kind, src, dst, dev, g):
        return pltpu.make_async_remote_copy(
            src_ref=src.at[g],
            dst_ref=dst.at[g],
            send_sem=send_sem.at[kind, g],
            recv_sem=recv_sem.at[kind, g],
            device_id=dev,
            device_id_type=MESH,
        )

    def near_copy(g):
        return send(NEAR, own_kv, near_kv, x_dev, g)

    def far_copy(g):
        return send(FAR, own_kv, far_kv, z_dev, g)

    def relay_copy(g):
        return send(RELAY, far_kv, relay_kv, x_dev, g)

    def near_back(g):
        return send(NEAR_BACK, near_send, near_recv, x_dev, g)

    def swap_copy(g):
        return send(SWAP, swap_send, swap_recv, x_dev, g)

    def far_back(g):
        return send(FAR_BACK, far_send, far_recv, z_dev, g)

    ahead = 3
    lead = 2
    flying = 2

    def around_copy(g):
        return send(RELAY, near_kv, relay_kv, z_dev, g)

    def other_back(g):
        return send(OTHER, swap_send, relay_kv, z_dev, g)

    def other_swap(g):
        return send(SWAP, relay_kv, swap_recv, x_dev, g)

    def by_early(g):
        return lax.rem(g, 8) == 5

    def back_apart(g):
        return lax.rem(g, 8) == 4

    def issue(g):
        far_copy(g).start()

        @pl.when(by_early(g))
        def _():
            near_copy(g).wait_recv()
            around_copy(g).start()

    @pl.when(early)
    def _():
        @pl.loop(0, groups)
        def _(g):
            @pl.when(by_early(g) | ((h == 0) & (g == 0)))
            def _():
                near_copy(g).start()

        @pl.loop(0, flying)
        def _(g):
            issue(g)

    @pl.when(late & (h == 0))
    def _():
        @pl.loop(0, ahead)
        def _(g):
            near_copy(g).start()

    def unit(g, blocks, diagonal, first):
        k = jnp.concatenate([kv[g, 0] for kv in blocks], 0)
        v = jnp.concatenate([kv[g, 1] for kv in blocks], 0)
        k_t = k.astype(F32).T.astype(BF16)
        keys = len(blocks) * rows
        lanes = pair * rows
        if diagonal:
            key_pos = lax.broadcasted_iota(jnp.int32, (keys, lanes), 0) - (keys - rows)
            query_pos = lax.broadcasted_iota(jnp.int32, (keys, lanes), 1) % rows
            allowed = key_pos <= query_pos
        probs_half = []
        dscores_half = []
        for t in range(ratio // pair):
            head = g * ratio + t * pair
            q = q_ref[pl.ds(head, pair)].reshape(lanes, width)
            go = g_ref[pl.ds(head, pair)].reshape(lanes, width)
            lse = jnp.concatenate([lse2[pl.ds(head + i, 1), :] for i in range(pair)], 1)
            delta = jnp.concatenate([delta_f[pl.ds(head + i, 1), :] for i in range(pair)], 1)
            probs = jnp.exp2(dot(k, q, NT) * (scale * LOG2E) - lse)
            if diagonal:
                probs = jnp.where(allowed, probs, 0.0)
            dprobs = dot(v, go, NT)
            dscores = (probs * (dprobs - delta)).astype(BF16)
            probs_half.append(probs.astype(BF16))
            dscores_half.append(dscores)
            dq_t = dot(k_t, dscores, NN)
            at = pl.ds(t * lanes, lanes)
            if first:
                dq_acc[g, :, at] = dq_t
            else:
                dq_acc[g, :, at] += dq_t
        at = pl.ds(g * ratio, ratio)
        q = q_ref[at].reshape(ratio * rows, width)
        go = g_ref[at].reshape(ratio * rows, width)
        dk = dot(jnp.concatenate(dscores_half, 1), q, NN) * scale
        dv = dot(jnp.concatenate(probs_half, 1), go, NN)
        return dk, dv

    def finish_dq(g):
        for i in range(ratio):
            dq_t = (dq_acc[g, :, pl.ds(i * rows, rows)] * scale).astype(BF16)
            dq_ref[g * ratio + i] = dq_t.T
        store_dq(g).start()

    def store_dq(g):
        at = pl.ds(g * ratio, ratio)
        return pltpu.make_async_copy(dq_ref.at[at], dq_hbm.at[at], store_sem.at[g])

    for load in loads[2:]:
        load.wait()
    lse2[...] = lse_ref[...].astype(F32) * LOG2E
    delta_f[...] = delta_ref[...].astype(F32)

    def near_unit(g):
        @pl.when(late | jnp.logical_not(by_early(g)))
        def _():
            near_copy(g).wait_recv()

        dk, dv = unit(g, [near_kv, own_kv], True, True)
        near_acc[g, 0] = dk[rows:]
        near_acc[g, 1] = dv[rows:]
        near_send[g, 0] = dk[:rows].astype(BF16)
        near_send[g, 1] = dv[:rows].astype(BF16)
        near_back(g).start()

    def near_step(g):
        @pl.when(h == 0)
        def _():
            dk, dv = unit(g, [own_kv], True, True)
            near_acc[g, 0] = dk
            near_acc[g, 1] = dv

        @pl.when(h == 1)
        def _():
            near_unit(g)

    @pl.when(early)
    def _():
        @pl.loop(0, groups)
        def _(g):
            far_copy(g).wait_send()

            @pl.when(by_early(g))
            def _():
                around_copy(g).wait_send()

            @pl.when(g + flying < groups)
            def _():
                issue(g + flying)

            @pl.when((h == 0) & (g + 1 < groups) & jnp.logical_not(by_early(g + 1)))
            def _():
                near_copy(g + 1).start()

            near_step(g)
            finish_dq(g)

    @pl.when(late)
    def _():
        @pl.loop(0, lead)
        def _(g):
            near_step(g)

    @pl.when(late)
    def _():
        @pl.loop(0, groups + 3)
        def _(t):
            @pl.when(t < groups)
            def _():
                far_copy(t).wait_recv()

                @pl.when(jnp.logical_not(by_early(t)))
                def _():
                    relay_copy(t).start()

                @pl.when((h == 0) & (t + ahead < groups))
                def _():
                    near_copy(t + ahead).start()

            @pl.when((t >= 1) & (t <= groups))
            def _():
                g = t - 1
                relay_copy(g).wait_recv()
                dk, dv = unit(g, [far_kv, relay_kv], False, False)
                swap_send[g, 0] = dk[rows:].astype(BF16)
                swap_send[g, 1] = dv[rows:].astype(BF16)

                @pl.when(back_apart(g))
                def _():
                    other_back(g).start()
                    far_send[g, 0] = dk[:rows].astype(BF16)
                    far_send[g, 1] = dv[:rows].astype(BF16)
                    far_back(g).start()

                @pl.when(jnp.logical_not(back_apart(g)))
                def _():
                    swap_copy(g).start()
                    far_acc[g, 0] = dk[:rows]
                    far_acc[g, 1] = dv[:rows]

                finish_dq(g)

            @pl.when(t + lead < groups)
            def _():
                near_step(t + lead)

            @pl.when((t >= 3) & jnp.logical_not(back_apart(t - 3)))
            def _():
                g = t - 3
                swap_copy(g).wait_recv()
                far_send[g] = (far_acc[g] + swap_recv[g].astype(F32)).astype(BF16)
                far_back(g).start()

    @pl.when(early)
    def _():
        @pl.loop(0, groups)
        def _(g):
            @pl.when(back_apart(g))
            def _():
                other_back(g).wait_recv()
                other_swap(g).start()

    @pl.loop(0, groups)
    def _(g):
        @pl.when(h == 0)
        def _():
            near_back(g).wait_recv()
            near_acc[g] += near_recv[g].astype(F32)

        @pl.when(early)
        def _():
            far_back(g).wait_recv()
            near_acc[g] += far_recv[g].astype(F32)

            @pl.when(back_apart(g))
            def _():
                other_swap(g).wait_recv()
                near_acc[g] += swap_recv[g].astype(F32)

        dk_ref[g] = near_acc[g, 0].astype(BF16)
        dv_ref[g] = near_acc[g, 1].astype(BF16)

    stores = [
        pltpu.make_async_copy(dk_ref, dk_hbm, load_sem.at[0]),
        pltpu.make_async_copy(dv_ref, dv_hbm, load_sem.at[1]),
    ]
    for store in stores:
        store.start()

    @pl.loop(0, groups)
    def _(g):
        store_dq(g).wait()

        @pl.when((h == 0) | (early & by_early(g)))
        def _():
            near_copy(g).wait_send()

        @pl.when(h == 1)
        def _():
            near_back(g).wait_send()

        @pl.when(early & back_apart(g))
        def _():
            other_swap(g).wait_send()

        @pl.when(late)
        def _():
            far_back(g).wait_send()

        @pl.when(late & jnp.logical_not(by_early(g)))
        def _():
            relay_copy(g).wait_send()

        @pl.when(late & back_apart(g))
        def _():
            other_back(g).wait_send()

        @pl.when(late & jnp.logical_not(back_apart(g)))
        def _():
            swap_copy(g).wait_send()

    for store in stores:
        store.wait()


def write_out(parts, *refs):
    count = len(parts)
    sources, results, staged = refs[:count], refs[count:2 * count], refs[2 * count:3 * count]
    read_sem, write_sem = refs[3 * count:]
    reads, writes = [], []
    for i, cuts in enumerate(parts):
        size = sources[i].shape[0] // cuts
        for j in range(cuts):
            at = pl.ds(j * size, size)
            n = len(reads)
            reads.append(
                pltpu.make_async_copy(sources[i].at[at], staged[i].at[at], read_sem.at[n])
            )
            writes.append(
                pltpu.make_async_copy(staged[i].at[at], results[i].at[at], write_sem.at[n])
            )
    for read in reads:
        read.start()
    for read, write in zip(reads, writes):
        read.wait()
        write.start()
    for write in writes:
        write.wait()


def local(queries, keys, values, delta, grad_out, lse):
    heads, rows, width = queries.shape
    groups = keys.shape[0]
    ratio = heads // groups
    n_ctx = lax.axis_size("ctx")
    block = (groups, 2, rows, width)
    anywhere = pl.BlockSpec(memory_space=pl.ANY)
    grads = pl.pallas_call(
        functools.partial(kernel, n_ctx),
        out_shape=(
            jax.ShapeDtypeStruct(queries.shape, BF16),
            jax.ShapeDtypeStruct(keys.shape, BF16),
            jax.ShapeDtypeStruct(values.shape, BF16),
        ),
        in_specs=[anywhere] * 6,
        out_specs=(anywhere,) * 3,
        scratch_shapes=[
            pltpu.VMEM(queries.shape, BF16),
            pltpu.VMEM(queries.shape, BF16),
            pltpu.VMEM(queries.shape, BF16),
            pltpu.VMEM(keys.shape, BF16),
            pltpu.VMEM(keys.shape, BF16),
            pltpu.VMEM(lse.shape, BF16),
            pltpu.VMEM(lse.shape, BF16),
            pltpu.VMEM((groups, width, ratio * rows), F32),
            pltpu.VMEM((heads, rows), F32),
            pltpu.VMEM((heads, rows), F32),
        ]
        + [pltpu.VMEM(block, BF16)] * 4
        + [pltpu.VMEM(block, F32)] * 2
        + [pltpu.VMEM(block, BF16)] * 6
        + [
            pltpu.SemaphoreType.DMA((6,)),
            pltpu.SemaphoreType.DMA((groups,)),
            pltpu.SemaphoreType.DMA((KINDS, groups)),
            pltpu.SemaphoreType.DMA((KINDS, groups)),
        ],
        compiler_params=pltpu.CompilerParams(
            collective_id=0, has_side_effects=True, vmem_limit_bytes=60 * 1024 * 1024
        ),
    )(queries, keys, values, delta, grad_out, lse)
    parts = (4, 1, 1)
    return pl.pallas_call(
        functools.partial(write_out, parts),
        out_shape=tuple(jax.ShapeDtypeStruct(x.shape, x.dtype) for x in grads),
        in_specs=[anywhere] * 3,
        out_specs=(anywhere,) * 3,
        scratch_shapes=[pltpu.VMEM(x.shape, x.dtype) for x in grads]
        + [pltpu.SemaphoreType.DMA((sum(parts),))] * 2,
        compiler_params=pltpu.CompilerParams(vmem_limit_bytes=60 * 1024 * 1024),
    )(*grads)


def solution(mesh):
    wide = P(None, ("ctx", "head"), None)
    flat = P(None, ("ctx", "head"))
    return jax.shard_map(
        local,
        mesh=mesh,
        in_specs=(wide, wide, wide, flat, wide, flat),
        out_specs=(wide, wide, wide),
        check_vma=False,
    )
```

```python
import functools
import math

import jax
import jax.numpy as jnp
from jax import lax
from jax.experimental import pallas as pl
from jax.experimental.pallas import tpu as pltpu
from jax.sharding import PartitionSpec as P

F32 = jnp.float32
BF16 = jnp.bfloat16
MESH = pl.DeviceIdType.MESH
LOG2E = 1.0 / math.log(2.0)
KINDS = 7
NEAR, FAR, RELAY, NEAR_BACK, SWAP, FAR_BACK, OTHER = range(KINDS)


def dot(a, b, dims):
    return lax.dot_general(a, b, (dims, ((), ())), preferred_element_type=F32)


NT = ((1,), (1,))
NN = ((1,), (0,))


def kernel(
    n_ctx,
    q_hbm, k_hbm, v_hbm, delta_hbm, g_hbm, lse_hbm,
    dq_hbm, dk_hbm, dv_hbm,
    q_ref, g_ref, dq_ref, dk_ref, dv_ref, lse_ref, delta_ref, dq_acc, lse2, delta_f,
    own_kv, near_kv, far_kv, relay_kv,
    near_acc, far_acc,
    near_send, near_recv, swap_send, swap_recv, far_send, far_recv,
    load_sem, store_sem, send_sem, recv_sem,
):
    groups, rows, width = k_hbm.shape
    heads = q_ref.shape[0]
    ratio = heads // groups
    pair = 2
    scale = 1.0 / math.sqrt(width)
    half = n_ctx // 2
    c = lax.axis_index("ctx")
    h = lax.axis_index("head")
    late = c >= half
    early = c < half
    x_dev = {"head": 1 - h}
    z_dev = {"ctx": lax.rem(c + half, n_ctx)}

    loads = [
        pltpu.make_async_copy(src, dst, load_sem.at[i])
        for i, (src, dst) in enumerate((
            (k_hbm, own_kv.at[:, 0]), (v_hbm, own_kv.at[:, 1]), (lse_hbm, lse_ref),
            (delta_hbm, delta_ref), (q_hbm, q_ref), (g_hbm, g_ref),
        ))
    ]
    for load in loads:
        load.start()

    barrier = pltpu.get_barrier_semaphore()
    for dev in (x_dev, z_dev):
        pl.semaphore_signal(barrier, inc=1, device_id=dev, device_id_type=MESH)
    loads[0].wait()
    loads[1].wait()
    pl.semaphore_wait(barrier, 2)

    def send(kind, src, dst, dev, g):
        return pltpu.make_async_remote_copy(
            src_ref=src.at[g],
            dst_ref=dst.at[g],
            send_sem=send_sem.at[kind, g],
            recv_sem=recv_sem.at[kind, g],
            device_id=dev,
            device_id_type=MESH,
        )

    def near_copy(g):
        return send(NEAR, own_kv, near_kv, x_dev, g)

    def far_copy(g):
        return send(FAR, own_kv, far_kv, z_dev, g)

    def relay_copy(g):
        return send(RELAY, far_kv, relay_kv, x_dev, g)

    def near_back(g):
        return send(NEAR_BACK, near_send, near_recv, x_dev, g)

    def swap_copy(g):
        return send(SWAP, swap_send, swap_recv, x_dev, g)

    def far_back(g):
        return send(FAR_BACK, far_send, far_recv, z_dev, g)

    ahead = 3
    lead = 2
    flying = jnp.where(c * 4 >= n_ctx, 4, 2)

    def around_copy(g):
        return send(RELAY, near_kv, relay_kv, z_dev, g)

    def other_back(g):
        return send(OTHER, swap_send, relay_kv, z_dev, g)

    def other_swap(g):
        return send(SWAP, relay_kv, swap_recv, x_dev, g)

    def by_early(g):
        return lax.rem(g, 3) == 2

    def back_apart(g):
        return lax.rem(g, 4) == 0

    def issue(g):
        far_copy(g).start()

        @pl.when(by_early(g))
        def _():
            near_copy(g).wait_recv()
            around_copy(g).start()

    @pl.when(early)
    def _():
        @pl.loop(0, groups)
        def _(g):
            @pl.when(by_early(g) | ((h == 0) & (g == 0)))
            def _():
                near_copy(g).start()

        @pl.loop(0, flying)
        def _(g):
            issue(g)

    @pl.when(late & (h == 0))
    def _():
        @pl.loop(0, ahead)
        def _(g):
            near_copy(g).start()

    def unit(g, blocks, diagonal, first):
        k = jnp.concatenate([kv[g, 0] for kv in blocks], 0)
        v = jnp.concatenate([kv[g, 1] for kv in blocks], 0)
        k_t = k.astype(F32).T.astype(BF16)
        keys = len(blocks) * rows
        lanes = pair * rows
        if diagonal:
            key_pos = lax.broadcasted_iota(jnp.int32, (keys, lanes), 0) - (keys - rows)
            query_pos = lax.broadcasted_iota(jnp.int32, (keys, lanes), 1) % rows
            allowed = key_pos <= query_pos
        probs_half = []
        dscores_half = []
        for t in range(ratio // pair):
            head = g * ratio + t * pair
            q = q_ref[pl.ds(head, pair)].reshape(lanes, width)
            go = g_ref[pl.ds(head, pair)].reshape(lanes, width)
            lse = jnp.concatenate([lse2[pl.ds(head + i, 1), :] for i in range(pair)], 1)
            delta = jnp.concatenate([delta_f[pl.ds(head + i, 1), :] for i in range(pair)], 1)
            probs = jnp.exp2(dot(k, q, NT) * (scale * LOG2E) - lse)
            if diagonal:
                probs = jnp.where(allowed, probs, 0.0)
            dprobs = dot(v, go, NT)
            dscores = (probs * (dprobs - delta)).astype(BF16)
            probs_half.append(probs.astype(BF16))
            dscores_half.append(dscores)
            dq_t = dot(k_t, dscores, NN)
            at = pl.ds(t * lanes, lanes)
            if first:
                dq_acc[g, :, at] = dq_t
            else:
                dq_acc[g, :, at] += dq_t
        at = pl.ds(g * ratio, ratio)
        q = q_ref[at].reshape(ratio * rows, width)
        go = g_ref[at].reshape(ratio * rows, width)
        dk = dot(jnp.concatenate(dscores_half, 1), q, NN) * scale
        dv = dot(jnp.concatenate(probs_half, 1), go, NN)
        return dk, dv

    def finish_dq(g):
        for i in range(ratio):
            dq_t = (dq_acc[g, :, pl.ds(i * rows, rows)] * scale).astype(BF16)
            dq_ref[g * ratio + i] = dq_t.T
        store_dq(g).start()

    def store_dq(g):
        at = pl.ds(g * ratio, ratio)
        return pltpu.make_async_copy(dq_ref.at[at], dq_hbm.at[at], store_sem.at[g])

    for load in loads[2:]:
        load.wait()
    lse2[...] = lse_ref[...].astype(F32) * LOG2E
    delta_f[...] = delta_ref[...].astype(F32)

    def near_unit(g):
        @pl.when(late | jnp.logical_not(by_early(g)))
        def _():
            near_copy(g).wait_recv()

        dk, dv = unit(g, [near_kv, own_kv], True, True)
        near_acc[g, 0] = dk[rows:]
        near_acc[g, 1] = dv[rows:]
        near_send[g, 0] = dk[:rows].astype(BF16)
        near_send[g, 1] = dv[:rows].astype(BF16)
        near_back(g).start()

    def near_step(g):
        @pl.when(h == 0)
        def _():
            dk, dv = unit(g, [own_kv], True, True)
            near_acc[g, 0] = dk
            near_acc[g, 1] = dv

        @pl.when(h == 1)
        def _():
            near_unit(g)

    @pl.when(early)
    def _():
        @pl.loop(0, groups)
        def _(g):
            far_copy(g).wait_send()

            @pl.when(by_early(g))
            def _():
                around_copy(g).wait_send()

            @pl.when(g + flying < groups)
            def _():
                issue(g + flying)

            @pl.when((h == 0) & (g + 1 < groups) & jnp.logical_not(by_early(g + 1)))
            def _():
                near_copy(g + 1).start()

            near_step(g)
            finish_dq(g)

    @pl.when(late)
    def _():
        @pl.loop(0, lead)
        def _(g):
            near_step(g)

    @pl.when(late)
    def _():
        @pl.loop(0, groups + 3)
        def _(t):
            @pl.when(t < groups)
            def _():
                far_copy(t).wait_recv()

                @pl.when(jnp.logical_not(by_early(t)))
                def _():
                    relay_copy(t).start()

                @pl.when((h == 0) & (t + ahead < groups))
                def _():
                    near_copy(t + ahead).start()

            @pl.when((t >= 1) & (t <= groups))
            def _():
                g = t - 1
                relay_copy(g).wait_recv()
                dk, dv = unit(g, [far_kv, relay_kv], False, False)
                swap_send[g, 0] = dk[rows:].astype(BF16)
                swap_send[g, 1] = dv[rows:].astype(BF16)

                @pl.when(back_apart(g))
                def _():
                    other_back(g).start()
                    far_send[g, 0] = dk[:rows].astype(BF16)
                    far_send[g, 1] = dv[:rows].astype(BF16)
                    far_back(g).start()

                @pl.when(jnp.logical_not(back_apart(g)))
                def _():
                    swap_copy(g).start()
                    far_acc[g, 0] = dk[:rows]
                    far_acc[g, 1] = dv[:rows]

                finish_dq(g)

            @pl.when(t + lead < groups)
            def _():
                near_step(t + lead)

            @pl.when((t >= 3) & jnp.logical_not(back_apart(t - 3)))
            def _():
                g = t - 3
                swap_copy(g).wait_recv()
                far_send[g] = (far_acc[g] + swap_recv[g].astype(F32)).astype(BF16)
                far_back(g).start()

    @pl.when(early)
    def _():
        @pl.loop(0, groups)
        def _(g):
            @pl.when(back_apart(g))
            def _():
                other_back(g).wait_recv()
                other_swap(g).start()

    @pl.loop(0, groups)
    def _(g):
        @pl.when(h == 0)
        def _():
            near_back(g).wait_recv()
            near_acc[g] += near_recv[g].astype(F32)

        @pl.when(early)
        def _():
            far_back(g).wait_recv()
            near_acc[g] += far_recv[g].astype(F32)

            @pl.when(back_apart(g))
            def _():
                other_swap(g).wait_recv()
                near_acc[g] += swap_recv[g].astype(F32)

        dk_ref[g] = near_acc[g, 0].astype(BF16)
        dv_ref[g] = near_acc[g, 1].astype(BF16)

    stores = [
        pltpu.make_async_copy(dk_ref, dk_hbm, load_sem.at[0]),
        pltpu.make_async_copy(dv_ref, dv_hbm, load_sem.at[1]),
    ]
    for store in stores:
        store.start()

    @pl.loop(0, groups)
    def _(g):
        store_dq(g).wait()

        @pl.when((h == 0) | (early & by_early(g)))
        def _():
            near_copy(g).wait_send()

        @pl.when(h == 1)
        def _():
            near_back(g).wait_send()

        @pl.when(early & back_apart(g))
        def _():
            other_swap(g).wait_send()

        @pl.when(late)
        def _():
            far_back(g).wait_send()

        @pl.when(late & jnp.logical_not(by_early(g)))
        def _():
            relay_copy(g).wait_send()

        @pl.when(late & back_apart(g))
        def _():
            other_back(g).wait_send()

        @pl.when(late & jnp.logical_not(back_apart(g)))
        def _():
            swap_copy(g).wait_send()

    for store in stores:
        store.wait()


def write_out(parts, *refs):
    count = len(parts)
    sources, results, staged = refs[:count], refs[count:2 * count], refs[2 * count:3 * count]
    read_sem, write_sem = refs[3 * count:]
    reads, writes = [], []
    for i, cuts in enumerate(parts):
        size = sources[i].shape[0] // cuts
        for j in range(cuts):
            at = pl.ds(j * size, size)
            n = len(reads)
            reads.append(
                pltpu.make_async_copy(sources[i].at[at], staged[i].at[at], read_sem.at[n])
            )
            writes.append(
                pltpu.make_async_copy(staged[i].at[at], results[i].at[at], write_sem.at[n])
            )
    for read in reads:
        read.start()
    for read, write in zip(reads, writes):
        read.wait()
        write.start()
    for write in writes:
        write.wait()


def local(queries, keys, values, delta, grad_out, lse):
    heads, rows, width = queries.shape
    groups = keys.shape[0]
    ratio = heads // groups
    n_ctx = lax.axis_size("ctx")
    block = (groups, 2, rows, width)
    anywhere = pl.BlockSpec(memory_space=pl.ANY)
    grads = pl.pallas_call(
        functools.partial(kernel, n_ctx),
        out_shape=(
            jax.ShapeDtypeStruct(queries.shape, BF16),
            jax.ShapeDtypeStruct(keys.shape, BF16),
            jax.ShapeDtypeStruct(values.shape, BF16),
        ),
        in_specs=[anywhere] * 6,
        out_specs=(anywhere,) * 3,
        scratch_shapes=[
            pltpu.VMEM(queries.shape, BF16),
            pltpu.VMEM(queries.shape, BF16),
            pltpu.VMEM(queries.shape, BF16),
            pltpu.VMEM(keys.shape, BF16),
            pltpu.VMEM(keys.shape, BF16),
            pltpu.VMEM(lse.shape, BF16),
            pltpu.VMEM(lse.shape, BF16),
            pltpu.VMEM((groups, width, ratio * rows), F32),
            pltpu.VMEM((heads, rows), F32),
            pltpu.VMEM((heads, rows), F32),
        ]
        + [pltpu.VMEM(block, BF16)] * 4
        + [pltpu.VMEM(block, F32)] * 2
        + [pltpu.VMEM(block, BF16)] * 6
        + [
            pltpu.SemaphoreType.DMA((6,)),
            pltpu.SemaphoreType.DMA((groups,)),
            pltpu.SemaphoreType.DMA((KINDS, groups)),
            pltpu.SemaphoreType.DMA((KINDS, groups)),
        ],
        compiler_params=pltpu.CompilerParams(
            collective_id=0, has_side_effects=True, vmem_limit_bytes=60 * 1024 * 1024
        ),
    )(queries, keys, values, delta, grad_out, lse)
    parts = (4, 1, 1)
    return pl.pallas_call(
        functools.partial(write_out, parts),
        out_shape=tuple(jax.ShapeDtypeStruct(x.shape, x.dtype) for x in grads),
        in_specs=[anywhere] * 3,
        out_specs=(anywhere,) * 3,
        scratch_shapes=[pltpu.VMEM(x.shape, x.dtype) for x in grads]
        + [pltpu.SemaphoreType.DMA((sum(parts),))] * 2,
        compiler_params=pltpu.CompilerParams(vmem_limit_bytes=60 * 1024 * 1024),
    )(*grads)


def solution(mesh):
    wide = P(None, ("ctx", "head"), None)
    flat = P(None, ("ctx", "head"))
    return jax.shard_map(
        local,
        mesh=mesh,
        in_specs=(wide, wide, wide, flat, wide, flat),
        out_specs=(wide, wide, wide),
        check_vma=False,
    )
```
